1024 devices in a mesh: op: 128 (over x, z), bond: 8 (over y, core).
Axes of the slice: x: 4, y: 4, z: 32, core: 2. Of those that a mesh axis runs over, the one named last changes fastest.
Arguments:
- left_env: bfloat16 [384, 32, 256, 256], P('op', 'bond'), may hold values from -6 to 6
- site_tensor: bfloat16 [32, 1024, 256], P('bond', 'op'), may hold values from -0.375 to 0.375
- sec_sizes: int32 [32], replicated, may hold values from 64 to 256, as said below
- coupling_values: float32 [384, 6], P('op'), may hold values from -4 to 4
- coupling_mask: int32 [384, 6], P('op'), may hold values 0 or 1
Outputs:
- new_env: bfloat16 [384, 32, 256, 256], P('op', 'bond')
The draws below stay inside these ranges and needn't reach their ends.
Inputs may be any that keep to these rules, and one draw needn't show every extreme that they name: `sec_sizes`: one sector has exactly 256 live rows in every draw.
All inputs are finite; a program needn't handle non-finite values. No bound on the sum of `coupling_mask` on one device may be relied on, other than what follows from the above.
Results may differ from the reference program's by a relative error of at most 0.0057.
Values may be sent and summed in bfloat16 or wider, within the bound.
A program may use at most 64 MiB of HBM per device.

```python
import jax
import jax.numpy as jnp
from jax import lax

SMAX = 256
PHYS = 4
NCOUP = 6
NSEC = 32
OPS = 384


def draw_sec_sizes(key, part):
    key = jax.random.fold_in(key, 11)
    first_key, second_key = jax.random.split(key)
    lengths = jax.random.randint(first_key, (NSEC,), SMAX // 4, SMAX + 1)
    chosen = jax.random.randint(second_key, (), 0, NSEC)
    return jnp.where(jnp.arange(NSEC) == chosen, SMAX, lengths).astype(jnp.int32)


def place_ends(drawn, own_key, least, largest):
    longest = drawn.shape.index(max(drawn.shape))
    spots = []
    for shift in (0, 1):
        where = [jax.random.randint(jax.random.fold_in(own_key, axis), (), 0, length) for axis, length in enumerate(drawn.shape)]
        where[longest] = (where[longest] + shift) % drawn.shape[longest]
        spots.append(tuple(where))
    return drawn.at[spots[0]].set(least).at[spots[1]].set(largest)


def steps_of(stream_key, shape, cuts, smallest, top_value):
    level, own = 1.0, jax.random.fold_in(stream_key, 6)
    for axis_at, shards_of in cuts:
        heights = jnp.exp(jax.random.uniform(jax.random.fold_in(own, axis_at), (shards_of,), jnp.float32, smallest / len(cuts), top_value / len(cuts)))
        level = level * jnp.repeat(heights, shape[axis_at] // shards_of).reshape([-1 if axis == axis_at else 1 for axis in range(len(shape))])
    return level


def noise(stream_key, shape, deviation, limit, shards=(), kind=jnp.bfloat16):
    gain = steps_of(stream_key, shape, shards, -0.22, 0.18) if shards else 1.0
    array = jax.random.normal(stream_key, shape, jnp.float32) * deviation * gain
    return jnp.minimum(jnp.maximum(array, -limit), limit).astype(kind)


def setup_inputs(seed: int = 0) -> dict:
    splits = jax.random.split(jax.random.key(seed), 6)
    return {
        "left_env": noise(splits[0], (OPS, NSEC, SMAX, SMAX), 1.0, 6.0, ((0, 128), (1, 8))),
        "site_tensor": noise(splits[1], (NSEC, PHYS * SMAX, SMAX), SMAX ** -0.5, 0.375, ((0, 8), (1, 128))),
        "sec_sizes": draw_sec_sizes(jax.random.fold_in(splits[5], 71), 0),
        "coupling_values": noise(splits[3], (OPS, NCOUP), 1.0, 4.0, ((0, 128),), jnp.float32),
        "coupling_mask": place_ends((jax.random.randint(splits[4], (OPS, NCOUP), 0, 4) < 3).astype(jnp.int32), jax.random.fold_in(splits[4], 1), 0, 1),
    }


CHANNELS = ((0, 1), (1, 3), (3, 4))


def keep_mask(lengths):
    positions = jnp.arange(SMAX, dtype=jnp.int32)
    return positions[None, :] < lengths[:, None]


def channel_term(environment, chosen, mixing):
    states = chosen.shape[1]
    mixed = []
    for p in range(states):
        summed = mixing[p, 0] * chosen[:, 0].astype(jnp.float32)
        for q in range(1, states):
            summed = summed + mixing[p, q] * chosen[:, q].astype(jnp.float32)
        mixed.append(summed)
    mixed = jnp.stack(mixed, 1).astype(jnp.bfloat16)
    product = jnp.einsum("mab,mpbc->mpac", environment.astype(jnp.float32), mixed.astype(jnp.float32),
                         precision=lax.Precision.HIGHEST).astype(jnp.bfloat16)
    return jnp.einsum("mpab,mpac->mbc", chosen.astype(jnp.float32), product.astype(jnp.float32),
                      precision=lax.Precision.HIGHEST)


def reference(left_env, site_tensor, sec_sizes, coupling_values, coupling_mask):
    blocks = site_tensor.reshape(NSEC, PHYS, SMAX, SMAX)
    padded = jnp.concatenate([sec_sizes, jnp.zeros((2,), jnp.int32)])
    row_keep = keep_mask(sec_sizes)
    chosen_all = []
    for n, (lower_state, upper_state) in enumerate(CHANNELS):
        col_keep = keep_mask(padded[n:n + NSEC])
        kept_mask = row_keep[:, None, :, None] & col_keep[:, None, None, :]
        chosen_all.append(jnp.where(kept_mask, blocks[:, lower_state:upper_state], jnp.zeros((), blocks.dtype)))
    env_keep = row_keep[:, :, None] & row_keep[:, None, :]
    coeffs = coupling_values * coupling_mask.astype(jnp.float32)

    def per_operator(operands):
        environment, coefficient = operands
        environment = jnp.where(env_keep, environment, jnp.zeros((), environment.dtype))
        mixings = (coefficient[0:1].reshape(1, 1), coefficient[1:5].reshape(2, 2), coefficient[5:6].reshape(1, 1))
        totals = jnp.zeros((NSEC, SMAX, SMAX), jnp.float32)
        for n in range(3):
            contribution = channel_term(environment, chosen_all[n], mixings[n])
            if n > 0:
                contribution = jnp.concatenate(
                    [jnp.zeros((n, SMAX, SMAX), jnp.float32), contribution[:NSEC - n]], 0)
            totals = totals + contribution
        return totals.astype(jnp.bfloat16)

    return lax.map(per_operator, (left_env, coeffs))
```

```python
import functools

import jax
import jax.numpy as jnp
from jax import lax
from jax.experimental import pallas as pl
from jax.experimental.pallas import tpu as pltpu
from jax.sharding import PartitionSpec as P

MESH = pl.DeviceIdType.MESH
NX, NZ, NB = 4, 32, 8
SLOTS, OPS, DIM = 4, 3, 256
ROOT = 15

PLAN = (
    (0, 15, (11, 19, 47, 110, 49, 14, 16, 45, 79, 111)),
    (0, 47, (48,)),
    (0, 14, (12, 46)),
    (0, 16, (18, 17, 112)),
    (0, 111, ()),
    (0, 110, (77, 109)),
    (0, 79, ()),
    (0, 49, (50, 81)),
    (0, 11, (7, 75, 10, 43, 107)),
    (0, 19, (27, 119, 20, 115)),
    (0, 45, ()),
    (0, 48, (78,)),
    (0, 46, ()),
    (0, 112, ()),
    (0, 17, ()),
    (0, 12, (44, 108)),
    (0, 18, (114,)),
    (0, 109, ()),
    (0, 77, (13, 76)),
    (0, 50, (82,)),
    (0, 81, (113,)),
    (0, 43, ()),
    (0, 10, (8, 9, 74, 42, 106)),
    (0, 20, (52, 53, 116)),
    (0, 107, ()),
    (0, 115, (117, 51, 83)),
    (0, 75, (73,)),
    (0, 44, ()),
    (0, 108, ()),
    (0, 7, (3, 39, 4, 103)),
    (0, 114, ()),
    (0, 78, (80,)),
    (0, 82, ()),
    (0, 76, ()),
    (0, 113, ()),
    (0, 13, ()),
    (0, 119, (120, 24, 22, 87, 55, 121, 23)),
    (0, 9, (105,)),
    (0, 106, ()),
    (0, 52, (84,)),
    (0, 116, ()),
    (0, 42, ()),
    (0, 8, (104,)),
    (0, 83, ()),
    (0, 73, (41, 72)),
    (0, 117, (21,)),
    (0, 74, ()),
    (0, 27, (30, 123, 28, 26, 61, 91, 59)),
    (0, 103, (101, 71)),
    (0, 39, (38,)),
    (0, 53, ()),
    (0, 51, ()),
    (0, 120, (88,)),
    (0, 87, (86,)),
    (0, 4, (36, 5, 100)),
    (0, 105, ()),
    (0, 80, ()),
    (0, 23, ()),
    (0, 3, (2, 97, 0, 99, 35)),
    (0, 104, ()),
    (0, 24, (56, 25)),
    (0, 84, (85,)),
    (0, 22, (54, 118)),
    (0, 121, ()),
    (0, 55, ()),
    (0, 41, (40,)),
    (0, 72, ()),
    (0, 21, ()),
    (0, 123, (124, 125)),
    (0, 28, (60,)),
    (0, 71, ()),
    (0, 38, (70, 6)),
    (0, 59, ()),
    (0, 26, (58, 122)),
    (0, 88, (89,)),
    (0, 101, (69,)),
    (0, 30, (126, 95, 63, 29, 31, 62)),
    (0, 91, ()),
    (0, 36, (37, 68)),
    (0, 86, ()),
    (0, 100, ()),
    (0, 5, ()),
    (0, 2, (1,)),
    (0, 56, (57,)),
    (0, 61, ()),
    (0, 35, (34, 67)),
    (0, 99, (66, 98)),
    (0, 25, ()),
    (0, 40, ()),
    (0, 54, ()),
    (0, 118, ()),
    (0, 85, ()),
    (0, 60, (92,)),
    (0, 124, (93,)),
    (0, 6, ()),
    (0, 70, (102,)),
    (0, 97, (64, 65, 96)),
    (0, 122, ()),
    (0, 58, ()),
    (0, 89, (90,)),
    (0, 0, (32,)),
    (0, 69, ()),
    (0, 125, ()),
    (0, 29, ()),
    (0, 126, (94, 127)),
    (0, 31, ()),
    (0, 62, ()),
    (0, 1, (33,)),
    (0, 37, ()),
    (0, 68, ()),
    (0, 34, ()),
    (0, 57, ()),
    (0, 98, ()),
    (0, 63, ()),
    (0, 67, ()),
    (0, 95, ()),
    (0, 92, ()),
    (0, 66, ()),
    (0, 102, ()),
    (0, 96, ()),
    (0, 90, ()),
    (0, 32, ()),
    (0, 65, ()),
    (0, 93, ()),
    (0, 64, ()),
    (0, 94, ()),
    (0, 127, ()),
    (0, 33, ()),
)


def offset(node):
    return (node // NZ, node % NZ - ROOT)


def kernel(
    groups, env_ref, site_ref, sizes_ref, values_ref, mask_ref, out_ref,
    bufs, stage, env, nat, tra, mixed,
    recv_sems, send_sems, own_send, own_recv, halo_send, halo_recv, env_sem,
):
    op, bond = lax.axis_index("op"), lax.axis_index("bond")
    x, z = op // NZ, op % NZ
    shift = (x + 1) // 2
    next_bond = lax.rem(bond + 1, NB)
    last_bond = lax.rem(bond + NB - 1, NB)
    lists = {(g, n): c for g, n, c in PLAN}

    def device(dx, dz, b):
        return (lax.rem(x + dx + 2 * NX, NX) * NZ + lax.rem(z + dz + 2 * NZ, NZ), b)

    first = sorted({c for g in range(len(groups)) for c in lists[(g, ROOT)]})
    barrier = pltpu.get_barrier_semaphore()
    pl.semaphore_signal(barrier, inc=1, device_id=(op, last_bond), device_id_type=MESH)
    for child in first:
        dx, dz = offset(child)
        pl.semaphore_signal(barrier, inc=1, device_id=device(-dx, -dz, bond), device_id_type=MESH)
        pl.semaphore_signal(barrier, inc=1, device_id=device(-dx, -dz, last_bond), device_id_type=MESH)

    own_env = pltpu.make_async_copy(env_ref, env.at[:, 2:6], env_sem)
    own_env.start()

    rows = lax.broadcasted_iota(jnp.int32, (8, DIM), 0) + z * 8
    cols = lax.broadcasted_iota(jnp.int32, (8, DIM), 1)
    for k in range(SLOTS):
        at = lax.rem(k - shift + SLOTS, SLOTS)
        left = bond * SLOTS + at
        right = left + shift
        height = sizes_ref[left]
        width = jnp.where(right < NB * SLOTS, sizes_ref[lax.rem(right, NB * SLOTS)], 0)
        block = site_ref[at].astype(jnp.float32)
        block = jnp.where((rows < height) & (cols < width), block, 0.0)
        stage[k] = jnp.concatenate([block[:, :128], block[:, 128:]], axis=0).astype(jnp.bfloat16)

    pl.semaphore_wait(barrier, 2 * len(first) + 1)

    def target_bond(k):
        return jnp.where(k < shift, next_bond, bond)

    def slot_of(k):
        for g, (lo, hi) in enumerate(groups):
            if lo <= k < hi:
                return g, k - lo

    for g, (lo, hi) in enumerate(groups):
        for child in lists[(g, ROOT)]:
            dx, dz = offset(child)
            parts = [(k, k + 1, target_bond(k)) for k in range(lo, min(hi, 2))]
            if hi > 2:
                parts.append((max(lo, 2), hi, bond))
            for a, b, t in parts:
                pltpu.make_async_remote_copy(
                    src_ref=stage.at[pl.ds(a, b - a)],
                    dst_ref=bufs[g].at[child, pl.ds(a - lo, b - a)],
                    send_sem=send_sems.at[g], recv_sem=recv_sems.at[g, child],
                    device_id=device(dx, dz, t), device_id_type=MESH,
                ).start()

    def own_copy(k):
        g, i = slot_of(k)
        return pltpu.make_async_remote_copy(
            src_ref=stage.at[k], dst_ref=bufs[g].at[ROOT, i],
            send_sem=own_send.at[k], recv_sem=own_recv.at[k],
            device_id=(op, next_bond), device_id_type=MESH,
        )

    halo = pltpu.make_async_remote_copy(
        src_ref=env_ref.at[:, 2:4], dst_ref=env.at[:, 0:2],
        send_sem=halo_send, recv_sem=halo_recv,
        device_id=(op, next_bond), device_id_type=MESH,
    )
    for k in range(2):
        @pl.when(k < shift)
        def _():
            own_copy(k).start()
    halo.start()
    for k in range(SLOTS):
        g, i = slot_of(k)
        if k < 2:
            @pl.when(k >= shift)
            def _():
                bufs[g][ROOT, i] = stage[k]
        else:
            bufs[g][ROOT, i] = stage[k]

    def copy(g, node, child):
        (ax, az), (bx, bz) = offset(node), offset(child)
        return pltpu.make_async_remote_copy(
            src_ref=bufs[g].at[node], dst_ref=bufs[g].at[child],
            send_sem=send_sems.at[g], recv_sem=recv_sems.at[g, child],
            device_id=device(bx - ax, bz - az, bond), device_id_type=MESH,
        )

    for g, node, children in PLAN:
        if node == ROOT:
            continue
        copy(g, node, node if not children else node).wait_recv()
        for child in children:
            copy(g, node, child).start()

    own_env.wait()
    for k in range(2):
        @pl.when(k < shift)
        def _():
            own_copy(k).wait_recv()
    halo.wait_recv()

    for k in range(SLOTS):
        g, i = slot_of(k)

        @pl.loop(0, NZ // 2)
        def _(m):
            for s in range(4):
                base = lax.rem(x - s + NX, NX) * NZ
                tiles = []
                for h in range(2):
                    j = lax.rem(z + ROOT - (2 * m + h) + 2 * NZ, NZ)
                    tiles.append(bufs[g][base + j, i].astype(jnp.float32))
                at = pl.ds(pl.multiple_of(m * 16, 16), 16)
                for half in range(2):
                    cut = slice(half * 8, half * 8 + 8)
                    nat[s, at, half * 128:half * 128 + 128] = jnp.concatenate(
                        [tiles[0][cut], tiles[1][cut]], axis=0).astype(jnp.bfloat16)

        for s in range(4):
            tra[:, s * DIM:(s + 1) * DIM] = nat[s].T
        for o in range(OPS):
            c = [values_ref[o, q] * mask_ref[o, q].astype(jnp.float32) for q in range(6)]

            def product(e, s):
                return jnp.dot(env[o, e], nat[s], preferred_element_type=jnp.float32)

            mixed[0:256] = (c[0] * product(k + 2, 0)).astype(jnp.bfloat16)
            one, two = product(k + 1, 1), product(k + 1, 2)
            mixed[256:512] = (c[1] * one + c[2] * two).astype(jnp.bfloat16)
            mixed[512:768] = (c[3] * one + c[4] * two).astype(jnp.bfloat16)
            mixed[768:1024] = (c[5] * product(k, 3)).astype(jnp.bfloat16)
            out_ref[o, k] = jnp.dot(tra[...], mixed[...], preferred_element_type=jnp.float32).astype(jnp.bfloat16)

    for k in range(2):
        @pl.when(k < shift)
        def _():
            own_copy(k).wait_send()
    halo.wait_send()
    for g in range(len(groups)):
        everything = bufs[g].at[pl.ds(0, NX * NZ - 1)]
        pltpu.make_async_remote_copy(
            src_ref=everything, dst_ref=everything, send_sem=send_sems.at[g], recv_sem=recv_sems.at[g, ROOT],
            device_id=(op, next_bond), device_id_type=MESH,
        ).wait_send()


GROUPS = ((0, 4),)


def body(groups, *refs):
    n = len(groups)
    ins, bufs, rest = refs[:6], refs[6:6 + n], refs[6 + n:]
    kernel(groups, *ins, bufs, *rest)


def local(left_env, site_tensor, sec_sizes, coupling_values, coupling_mask):
    return pl.pallas_call(
        functools.partial(body, GROUPS),
        name="gather_and_renormalize",
        out_shape=jax.ShapeDtypeStruct(left_env.shape, jnp.bfloat16),
        in_specs=[
            pl.BlockSpec(memory_space=pl.ANY),
            pl.BlockSpec(memory_space=pltpu.VMEM),
            pl.BlockSpec(memory_space=pltpu.SMEM),
            pl.BlockSpec(memory_space=pltpu.SMEM),
            pl.BlockSpec(memory_space=pltpu.SMEM),
        ],
        out_specs=pl.BlockSpec(memory_space=pltpu.VMEM),
        scratch_shapes=[pltpu.VMEM((NX * NZ, hi - lo, 16, 128), jnp.bfloat16) for lo, hi in GROUPS] + [
            pltpu.VMEM((SLOTS, 16, 128), jnp.bfloat16),
            pltpu.VMEM((OPS, 6, DIM, DIM), jnp.bfloat16),
            pltpu.VMEM((4, DIM, DIM), jnp.bfloat16),
            pltpu.VMEM((DIM, 4 * DIM), jnp.bfloat16),
            pltpu.VMEM((4 * DIM, DIM), jnp.bfloat16),
            pltpu.SemaphoreType.DMA((len(GROUPS), NX * NZ)),
            pltpu.SemaphoreType.DMA((len(GROUPS),)),
            pltpu.SemaphoreType.DMA((2,)),
            pltpu.SemaphoreType.DMA((2,)),
            pltpu.SemaphoreType.DMA,
            pltpu.SemaphoreType.DMA,
            pltpu.SemaphoreType.DMA,
        ],
        compiler_params=pltpu.CompilerParams(
            collective_id=0, has_side_effects=True, vmem_limit_bytes=60 * 1024 * 1024
        ),
        cost_estimate=pl.CostEstimate(flops=3_221_225_472, bytes_accessed=3_145_728, transcendentals=0),
    )(left_env, site_tensor, sec_sizes, coupling_values, coupling_mask)


def solution(mesh):
    placed = (P("op", "bond", None, None), P("bond", "op", None), P(), P("op", None), P("op", None))
    return jax.shard_map(
        local, mesh=mesh, in_specs=placed, out_specs=P("op", "bond", None, None), check_vma=False
    )
```

```python
import jax
import jax.numpy as jnp
from jax import lax
from jax.experimental import pallas as pl
from jax.experimental.pallas import tpu as pltpu
from jax.sharding import PartitionSpec as P

MESH = pl.DeviceIdType.MESH
NX, NZ, NB = 4, 32, 8
SLOTS, OPS, DIM = 4, 3, 256
ROOT = 15

PLAN = (
    (0, 15, (11, 19, 47, 110, 49, 14, 16, 45, 79, 111)),
    (0, 47, (48,)),
    (0, 14, (12, 46)),
    (0, 16, (18, 17, 112)),
    (0, 111, ()),
    (0, 110, (77, 109)),
    (0, 79, ()),
    (0, 49, (50, 81)),
    (0, 11, (7, 75, 10, 43, 107)),
    (0, 19, (27, 119, 20, 115)),
    (0, 45, ()),
    (0, 48, (78,)),
    (0, 46, ()),
    (0, 112, ()),
    (0, 17, ()),
    (0, 12, (44, 108)),
    (0, 18, (114,)),
    (0, 109, ()),
    (0, 77, (13, 76)),
    (0, 50, (82,)),
    (0, 81, (113,)),
    (0, 43, ()),
    (0, 10, (8, 9, 74, 42, 106)),
    (0, 20, (52, 53, 116)),
    (0, 107, ()),
    (0, 115, (117, 51, 83)),
    (0, 75, (73,)),
    (0, 44, ()),
    (0, 108, ()),
    (0, 7, (3, 39, 4, 103)),
    (0, 114, ()),
    (0, 78, (80,)),
    (0, 82, ()),
    (0, 76, ()),
    (0, 113, ()),
    (0, 13, ()),
    (0, 119, (120, 24, 22, 87, 55, 121, 23)),
    (0, 9, (105,)),
    (0, 106, ()),
    (0, 52, (84,)),
    (0, 116, ()),
    (0, 42, ()),
    (0, 8, (104,)),
    (0, 83, ()),
    (0, 73, (41, 72)),
    (0, 117, (21,)),
    (0, 74, ()),
    (0, 27, (30, 123, 28, 26, 61, 91, 59)),
    (0, 103, (101, 71)),
    (0, 39, (38,)),
    (0, 53, ()),
    (0, 51, ()),
    (0, 120, (88,)),
    (0, 87, (86,)),
    (0, 4, (36, 5, 100)),
    (0, 105, ()),
    (0, 80, ()),
    (0, 23, ()),
    (0, 3, (2, 97, 0, 99, 35)),
    (0, 104, ()),
    (0, 24, (56, 25)),
    (0, 84, (85,)),
    (0, 22, (54, 118)),
    (0, 121, ()),
    (0, 55, ()),
    (0, 41, (40,)),
    (0, 72, ()),
    (0, 21, ()),
    (0, 123, (124, 125)),
    (0, 28, (60,)),
    (0, 71, ()),
    (0, 38, (70, 6)),
    (0, 59, ()),
    (0, 26, (58, 122)),
    (0, 88, (89,)),
    (0, 101, (69,)),
    (0, 30, (126, 95, 63, 29, 31, 62)),
    (0, 91, ()),
    (0, 36, (37, 68)),
    (0, 86, ()),
    (0, 100, ()),
    (0, 5, ()),
    (0, 2, (1,)),
    (0, 56, (57,)),
    (0, 61, ()),
    (0, 35, (34, 67)),
    (0, 99, (66, 98)),
    (0, 25, ()),
    (0, 40, ()),
    (0, 54, ()),
    (0, 118, ()),
    (0, 85, ()),
    (0, 60, (92,)),
    (0, 124, (93,)),
    (0, 6, ()),
    (0, 70, (102,)),
    (0, 97, (64, 65, 96)),
    (0, 122, ()),
    (0, 58, ()),
    (0, 89, (90,)),
    (0, 0, (32,)),
    (0, 69, ()),
    (0, 125, ()),
    (0, 29, ()),
    (0, 126, (94, 127)),
    (0, 31, ()),
    (0, 62, ()),
    (0, 1, (33,)),
    (0, 37, ()),
    (0, 68, ()),
    (0, 34, ()),
    (0, 57, ()),
    (0, 98, ()),
    (0, 63, ()),
    (0, 67, ()),
    (0, 95, ()),
    (0, 92, ()),
    (0, 66, ()),
    (0, 102, ()),
    (0, 96, ()),
    (0, 90, ()),
    (0, 32, ()),
    (0, 65, ()),
    (0, 93, ()),
    (0, 64, ()),
    (0, 94, ()),
    (0, 127, ()),
    (0, 33, ()),
)


def offset(node):
    return (node // NZ, node % NZ - ROOT)


def gather(
    env_ref, site_in, sizes_in, buf, halo_ref,
    stage, site_ref, sizes_ref,
    recv_sems, leaf_sems, send_sem, own_send, own_recv, halo_send, halo_recv, in_sems,
):
    op, bond = lax.axis_index("op"), lax.axis_index("bond")
    x, z = op // NZ, op % NZ
    shift = (x + 1) // 2
    next_bond = lax.rem(bond + 1, NB)
    last_bond = lax.rem(bond + NB - 1, NB)
    lists = {n: c for _, n, c in PLAN}

    def device(dx, dz, b):
        return (lax.rem(x + dx + 2 * NX, NX) * NZ + lax.rem(z + dz + 2 * NZ, NZ), b)

    first = sorted(lists[ROOT])
    barrier = pltpu.get_barrier_semaphore()
    pl.semaphore_signal(barrier, inc=1, device_id=(op, last_bond), device_id_type=MESH)
    for child in first:
        dx, dz = offset(child)
        pl.semaphore_signal(barrier, inc=1, device_id=device(-dx, -dz, bond), device_id_type=MESH)
        pl.semaphore_signal(barrier, inc=1, device_id=device(-dx, -dz, last_bond), device_id_type=MESH)

    site_copy = pltpu.make_async_copy(site_in, site_ref, in_sems.at[0])
    sizes_copy = pltpu.make_async_copy(sizes_in, sizes_ref, in_sems.at[1])
    for c in (site_copy, sizes_copy):
        c.start()
    site_copy.wait()
    sizes_copy.wait()

    rows = lax.broadcasted_iota(jnp.int32, (8, DIM), 0) + z * 8
    cols = lax.broadcasted_iota(jnp.int32, (8, DIM), 1)
    for k in range(SLOTS):
        at = lax.rem(k - shift + SLOTS, SLOTS)
        left = bond * SLOTS + at
        right = left + shift
        height = sizes_ref[left]
        width = jnp.where(right < NB * SLOTS, sizes_ref[lax.rem(right, NB * SLOTS)], 0)
        block = site_ref[at].astype(jnp.float32)
        block = jnp.where((rows < height) & (cols < width), block, 0.0)
        stage[k] = jnp.concatenate([block[:, :128], block[:, 128:]], axis=0).astype(jnp.bfloat16)

    pl.semaphore_wait(barrier, 2 * len(first) + 1)

    def target_bond(k):
        return jnp.where(k < shift, next_bond, bond)

    def arrival(child):
        return recv_sems.at[child] if lists[child] else leaf_sems.at[child // NZ]

    for child in lists[ROOT]:
        dx, dz = offset(child)
        for lo, hi, to in ((0, 1, target_bond(0)), (1, 2, target_bond(1)), (2, SLOTS, bond)):
            pltpu.make_async_remote_copy(
                src_ref=stage.at[pl.ds(lo, hi - lo)],
                dst_ref=buf.at[child, pl.ds(lo, hi - lo)],
                send_sem=send_sem, recv_sem=arrival(child),
                device_id=device(dx, dz, to), device_id_type=MESH,
            ).start()

    def own_copy(k):
        return pltpu.make_async_remote_copy(
            src_ref=stage.at[k], dst_ref=buf.at[ROOT, k],
            send_sem=own_send.at[k], recv_sem=own_recv.at[k],
            device_id=(op, next_bond), device_id_type=MESH,
        )

    halo = pltpu.make_async_remote_copy(
        src_ref=env_ref.at[:, 2:4], dst_ref=halo_ref,
        send_sem=halo_send, recv_sem=halo_recv,
        device_id=(op, next_bond), device_id_type=MESH,
    )
    for k in range(SLOTS):
        if k < 2:
            @pl.when(k < shift)
            def _():
                own_copy(k).start()

            @pl.when(k >= shift)
            def _():
                buf[ROOT, k] = stage[k]
        else:
            buf[ROOT, k] = stage[k]
    halo.start()

    def copy(node, child):
        (ax, az), (bx, bz) = offset(node), offset(child)
        return pltpu.make_async_remote_copy(
            src_ref=buf.at[node], dst_ref=buf.at[child],
            send_sem=send_sem, recv_sem=arrival(child),
            device_id=device(bx - ax, bz - az, bond), device_id_type=MESH,
        )

    for _, node, children in PLAN:
        if node != ROOT and children:
            copy(node, node).wait_recv()
            for child in children:
                copy(node, child).start()

    for k in range(2):
        @pl.when(k < shift)
        def _():
            own_copy(k).wait_recv()

    for ox in range(NX):
        leaves = sum(1 for n, c in lists.items() if n // NZ == ox and not c)
        if leaves:
            some = buf.at[pl.ds(0, leaves)]
            pltpu.make_async_remote_copy(
                src_ref=some, dst_ref=some, send_sem=send_sem, recv_sem=leaf_sems.at[ox],
                device_id=(op, next_bond), device_id_type=MESH,
            ).wait_recv()
    halo.wait_recv()
    for k in range(2):
        @pl.when(k < shift)
        def _():
            own_copy(k).wait_send()
    halo.wait_send()
    everything = buf.at[pl.ds(0, NX * NZ - 1)]
    pltpu.make_async_remote_copy(
        src_ref=everything, dst_ref=everything, send_sem=send_sem, recv_sem=halo_recv,
        device_id=(op, next_bond), device_id_type=MESH,
    ).wait_send()


def products(own, buf, halo, values_ref, mask_ref, out_ref, nat, tra, mixed, result, sems):
    op = lax.axis_index("op")
    x, z = op // NZ, op % NZ
    tile = [lax.rem(z + ROOT - m + NZ, NZ) for m in range(NZ)]
    plane = [lax.rem(x - s + NX, NX) * NZ for s in range(4)]
    for k in range(SLOTS):
        for s in range(4):
            tiles = [buf[plane[s] + j, k].astype(jnp.float32) for j in tile]
            left = jnp.concatenate([t[:8] for t in tiles], axis=0)
            right = jnp.concatenate([t[8:] for t in tiles], axis=0)
            block = jnp.concatenate([left, right], axis=1).astype(jnp.bfloat16)
            nat[k, s] = block
            tra[k, :, s * DIM:(s + 1) * DIM] = block.T

    def env(o, e):
        return own[o, e] if e >= 0 else halo[o, e + 2]

    copies = []
    for k in range(SLOTS):
        for o in range(OPS):
            c = [values_ref[o, q] * mask_ref[o, q].astype(jnp.float32) for q in range(6)]

            def product(e, s):
                return jnp.dot(env(o, e), nat[k, s], preferred_element_type=jnp.float32)

            mixed[o, 0:256] = (c[0] * product(k, 0)).astype(jnp.bfloat16)
            one, two = product(k - 1, 1), product(k - 1, 2)
            mixed[o, 256:512] = (c[1] * one + c[2] * two).astype(jnp.bfloat16)
            mixed[o, 512:768] = (c[3] * one + c[4] * two).astype(jnp.bfloat16)
            mixed[o, 768:1024] = (c[5] * product(k - 2, 3)).astype(jnp.bfloat16)
            result[o, k] = jnp.dot(tra[k], mixed[o], preferred_element_type=jnp.float32).astype(jnp.bfloat16)
            copies.append(pltpu.make_async_copy(result.at[o, k], out_ref.at[o, k], sems.at[o, k]))
            copies[-1].start()
    for copy in copies:
        copy.wait()


VMEM, SMEM, ANY, HBM = (pl.BlockSpec(memory_space=m) for m in (pltpu.VMEM, pltpu.SMEM, pl.ANY, pltpu.HBM))


def local(left_env, site_tensor, sec_sizes, coupling_values, coupling_mask):
    buf, halo = pl.pallas_call(
        gather,
        name="gather",
        out_shape=[
            pltpu.VMEM((NX * NZ, SLOTS, 16, 128), jnp.bfloat16),
            pltpu.VMEM((OPS, 2, DIM, DIM), jnp.bfloat16),
        ],
        in_specs=[HBM] * 3,
        out_specs=[VMEM] * 2,
        scratch_shapes=[
            pltpu.VMEM((SLOTS, 16, 128), jnp.bfloat16),
            pltpu.VMEM((SLOTS, 8, DIM), jnp.bfloat16),
            pltpu.SMEM((NB * SLOTS,), jnp.int32),
            pltpu.SemaphoreType.DMA((NX * NZ,)),
            pltpu.SemaphoreType.DMA((NX,)),
            pltpu.SemaphoreType.DMA,
            pltpu.SemaphoreType.DMA((2,)),
            pltpu.SemaphoreType.DMA((2,)),
            pltpu.SemaphoreType.DMA,
            pltpu.SemaphoreType.DMA,
            pltpu.SemaphoreType.DMA((2,)),
        ],
        compiler_params=pltpu.CompilerParams(
            collective_id=0, has_side_effects=True, vmem_limit_bytes=56 * 1024 * 1024
        ),
        cost_estimate=pl.CostEstimate(flops=0, bytes_accessed=6_000_000, transcendentals=0),
    )(left_env, site_tensor, sec_sizes)
    return pl.pallas_call(
        products,
        name="products",
        out_shape=jax.ShapeDtypeStruct(left_env.shape, jnp.bfloat16),
        in_specs=[VMEM, VMEM, VMEM, SMEM, SMEM],
        out_specs=HBM,
        scratch_shapes=[
            pltpu.VMEM((SLOTS, 4, DIM, DIM), jnp.bfloat16),
            pltpu.VMEM((SLOTS, DIM, 4 * DIM), jnp.bfloat16),
            pltpu.VMEM((OPS, 4 * DIM, DIM), jnp.bfloat16),
            pltpu.VMEM((OPS, SLOTS, DIM, DIM), jnp.bfloat16),
            pltpu.SemaphoreType.DMA((OPS, SLOTS)),
        ],
        compiler_params=pltpu.CompilerParams(vmem_limit_bytes=32 * 1024 * 1024),
        cost_estimate=pl.CostEstimate(flops=3_221_225_472, bytes_accessed=3_145_728, transcendentals=0),
    )(left_env, buf, halo, coupling_values, coupling_mask)


def solution(mesh):
    placed = (P("op", "bond", None, None), P("bond", "op", None), P(), P("op", None), P("op", None))
    return jax.shard_map(
        local, mesh=mesh, in_specs=placed, out_specs=P("op", "bond", None, None), check_vma=False
    )
```

```python
import jax
import jax.numpy as jnp
from jax import lax
from jax.experimental import pallas as pl
from jax.experimental.pallas import tpu as pltpu
from jax.sharding import PartitionSpec as P

MESH = pl.DeviceIdType.MESH
NX, NZ, NB = 4, 32, 8
SLOTS, OPS, DIM = 4, 3, 256
ROOT = 15

PLAN = (
    (0, 15, (11, 19, 47, 110, 49, 14, 16, 45, 79, 111)),
    (0, 47, (48,)),
    (0, 14, (12, 46)),
    (0, 16, (18, 17, 112)),
    (0, 111, ()),
    (0, 110, (77, 109)),
    (0, 79, ()),
    (0, 49, (50, 81)),
    (0, 11, (7, 75, 10, 43, 107)),
    (0, 19, (27, 119, 20, 115)),
    (0, 45, ()),
    (0, 48, (78,)),
    (0, 46, ()),
    (0, 112, ()),
    (0, 17, ()),
    (0, 12, (44, 108)),
    (0, 18, (114,)),
    (0, 109, ()),
    (0, 77, (13, 76)),
    (0, 50, (82,)),
    (0, 81, (113,)),
    (0, 43, ()),
    (0, 10, (8, 9, 74, 42, 106)),
    (0, 20, (52, 53, 116)),
    (0, 107, ()),
    (0, 115, (117, 51, 83)),
    (0, 75, (73,)),
    (0, 44, ()),
    (0, 108, ()),
    (0, 7, (3, 39, 4, 103)),
    (0, 114, ()),
    (0, 78, (80,)),
    (0, 82, ()),
    (0, 76, ()),
    (0, 113, ()),
    (0, 13, ()),
    (0, 119, (120, 24, 22, 87, 55, 121, 23)),
    (0, 9, (105,)),
    (0, 106, ()),
    (0, 52, (84,)),
    (0, 116, ()),
    (0, 42, ()),
    (0, 8, (104,)),
    (0, 83, ()),
    (0, 73, (41, 72)),
    (0, 117, (21,)),
    (0, 74, ()),
    (0, 27, (30, 123, 28, 26, 61, 91, 59)),
    (0, 103, (101, 71)),
    (0, 39, (38,)),
    (0, 53, ()),
    (0, 51, ()),
    (0, 120, (88,)),
    (0, 87, (86,)),
    (0, 4, (36, 5, 100)),
    (0, 105, ()),
    (0, 80, ()),
    (0, 23, ()),
    (0, 3, (2, 97, 0, 99, 35)),
    (0, 104, ()),
    (0, 24, (56, 25)),
    (0, 84, (85,)),
    (0, 22, (54, 118)),
    (0, 121, ()),
    (0, 55, ()),
    (0, 41, (40,)),
    (0, 72, ()),
    (0, 21, ()),
    (0, 123, (124, 125)),
    (0, 28, (60,)),
    (0, 71, ()),
    (0, 38, (70, 6)),
    (0, 59, ()),
    (0, 26, (58, 122)),
    (0, 88, (89,)),
    (0, 101, (69,)),
    (0, 30, (126, 95, 63, 29, 31, 62)),
    (0, 91, ()),
    (0, 36, (37, 68)),
    (0, 86, ()),
    (0, 100, ()),
    (0, 5, ()),
    (0, 2, (1,)),
    (0, 56, (57,)),
    (0, 61, ()),
    (0, 35, (34, 67)),
    (0, 99, (66, 98)),
    (0, 25, ()),
    (0, 40, ()),
    (0, 54, ()),
    (0, 118, ()),
    (0, 85, ()),
    (0, 60, (92,)),
    (0, 124, (93,)),
    (0, 6, ()),
    (0, 70, (102,)),
    (0, 97, (64, 65, 96)),
    (0, 122, ()),
    (0, 58, ()),
    (0, 89, (90,)),
    (0, 0, (32,)),
    (0, 69, ()),
    (0, 125, ()),
    (0, 29, ()),
    (0, 126, (94, 127)),
    (0, 31, ()),
    (0, 62, ()),
    (0, 1, (33,)),
    (0, 37, ()),
    (0, 68, ()),
    (0, 34, ()),
    (0, 57, ()),
    (0, 98, ()),
    (0, 63, ()),
    (0, 67, ()),
    (0, 95, ()),
    (0, 92, ()),
    (0, 66, ()),
    (0, 102, ()),
    (0, 96, ()),
    (0, 90, ()),
    (0, 32, ()),
    (0, 65, ()),
    (0, 93, ()),
    (0, 64, ()),
    (0, 94, ()),
    (0, 127, ()),
    (0, 33, ()),
)


def offset(node):
    return (node // NZ, node % NZ - ROOT)


def gather(
    env_ref, site_in, sizes_in, buf, halo_ref,
    stage, site_ref, sizes_ref,
    recv_sems, leaf_sems, send_sem, own_send, own_recv, halo_send, halo_recv, in_sems,
):
    op, bond = lax.axis_index("op"), lax.axis_index("bond")
    x, z = op // NZ, op % NZ
    shift = (x + 1) // 2
    next_bond = lax.rem(bond + 1, NB)
    last_bond = lax.rem(bond + NB - 1, NB)
    lists = {n: c for _, n, c in PLAN}

    def device(dx, dz, b):
        return (lax.rem(x + dx + 2 * NX, NX) * NZ + lax.rem(z + dz + 2 * NZ, NZ), b)

    first = sorted(lists[ROOT], key=lambda c: -abs(offset(c)[1]))
    barrier = pltpu.get_barrier_semaphore()
    for child in first:
        dx, dz = offset(child)
        for b in (last_bond, bond):
            pl.semaphore_signal(barrier, inc=1, device_id=device(-dx, -dz, b), device_id_type=MESH)
    pl.semaphore_signal(barrier, inc=1, device_id=(op, last_bond), device_id_type=MESH)

    site_copy = pltpu.make_async_copy(site_in, site_ref, in_sems.at[0])
    sizes_copy = pltpu.make_async_copy(sizes_in, sizes_ref, in_sems.at[1])
    for c in (site_copy, sizes_copy):
        c.start()
    site_copy.wait()
    sizes_copy.wait()

    rows = lax.broadcasted_iota(jnp.int32, (8, DIM), 0) + z * 8
    cols = lax.broadcasted_iota(jnp.int32, (8, DIM), 1)
    for k in range(SLOTS):
        at = lax.rem(k - shift + SLOTS, SLOTS)
        left = bond * SLOTS + at
        right = left + shift
        height = sizes_ref[left]
        width = jnp.where(right < NB * SLOTS, sizes_ref[lax.rem(right, NB * SLOTS)], 0)
        block = site_ref[at].astype(jnp.float32)
        block = jnp.where((rows < height) & (cols < width), block, 0.0)
        stage[k] = jnp.concatenate([block[:, :128], block[:, 128:]], axis=0).astype(jnp.bfloat16)

    pl.semaphore_wait(barrier, 2 * len(first) + 1)

    def arrival(child):
        return recv_sems.at[child] if lists[child] else leaf_sems.at[child // NZ]

    for moved in range(3):
        @pl.when(shift == moved)
        def _():
            for child in lists[ROOT]:
                dx, dz = offset(child)
                for lo, hi, to in ((0, moved, next_bond), (moved, SLOTS, bond)):
                    if lo < hi:
                        pltpu.make_async_remote_copy(
                            src_ref=stage.at[pl.ds(lo, hi - lo)],
                            dst_ref=buf.at[child, pl.ds(lo, hi - lo)],
                            send_sem=send_sem, recv_sem=arrival(child),
                            device_id=device(dx, dz, to), device_id_type=MESH,
                        ).start()

    def own_copy(k):
        return pltpu.make_async_remote_copy(
            src_ref=stage.at[k], dst_ref=buf.at[ROOT, k],
            send_sem=own_send.at[k], recv_sem=own_recv.at[k],
            device_id=(op, next_bond), device_id_type=MESH,
        )

    halo = pltpu.make_async_remote_copy(
        src_ref=env_ref.at[:, 2:4], dst_ref=halo_ref,
        send_sem=halo_send, recv_sem=halo_recv,
        device_id=(op, next_bond), device_id_type=MESH,
    )
    for k in range(SLOTS):
        if k < 2:
            @pl.when(k < shift)
            def _():
                own_copy(k).start()

            @pl.when(k >= shift)
            def _():
                buf[ROOT, k] = stage[k]
        else:
            buf[ROOT, k] = stage[k]
    halo.start()

    def copy(node, child):
        (ax, az), (bx, bz) = offset(node), offset(child)
        return pltpu.make_async_remote_copy(
            src_ref=buf.at[node], dst_ref=buf.at[child],
            send_sem=send_sem, recv_sem=arrival(child),
            device_id=device(bx - ax, bz - az, bond), device_id_type=MESH,
        )

    for _, node, children in PLAN:
        if node != ROOT and children:
            copy(node, node).wait_recv()
            for child in children:
                copy(node, child).start()

    for k in range(2):
        @pl.when(k < shift)
        def _():
            own_copy(k).wait_recv()

    for ox in range(NX):
        leaves = sum(1 for n, c in lists.items() if n // NZ == ox and not c)
        if leaves:
            some = buf.at[pl.ds(0, leaves)]
            pltpu.make_async_remote_copy(
                src_ref=some, dst_ref=some, send_sem=send_sem, recv_sem=leaf_sems.at[ox],
                device_id=(op, next_bond), device_id_type=MESH,
            ).wait_recv()
    halo.wait_recv()
    for k in range(2):
        @pl.when(k < shift)
        def _():
            own_copy(k).wait_send()
    halo.wait_send()
    everything = buf.at[pl.ds(0, NX * NZ - 1)]
    pltpu.make_async_remote_copy(
        src_ref=everything, dst_ref=everything, send_sem=send_sem, recv_sem=halo_recv,
        device_id=(op, next_bond), device_id_type=MESH,
    ).wait_send()


def products(own, buf, halo, values_ref, mask_ref, out_ref, nat, tra, mixed, result, sems):
    op = lax.axis_index("op")
    x, z = op // NZ, op % NZ
    tile = [lax.rem(z + ROOT - m + NZ, NZ) for m in range(NZ)]
    plane = [lax.rem(x - s + NX, NX) * NZ for s in range(4)]
    for k in range(SLOTS):
        for s in range(4):
            tiles = [buf[plane[s] + j, k].astype(jnp.float32) for j in tile]
            left = jnp.concatenate([t[:8] for t in tiles], axis=0)
            right = jnp.concatenate([t[8:] for t in tiles], axis=0)
            block = jnp.concatenate([left, right], axis=1).astype(jnp.bfloat16)
            nat[k, s] = block
            tra[k, :, s * DIM:(s + 1) * DIM] = block.T

    def env(o, e):
        return own[o, e] if e >= 0 else halo[o, e + 2]

    def mix(k, o, at):
        c = [values_ref[o, q] * mask_ref[o, q].astype(jnp.float32) for q in range(6)]

        def product(e, s):
            return jnp.dot(env(o, e), nat[k, s], preferred_element_type=jnp.float32)

        mixed[at, 0:256] = (c[0] * product(k, 0)).astype(jnp.bfloat16)
        one, two = product(k - 1, 1), product(k - 1, 2)
        mixed[at, 256:512] = (c[1] * one + c[2] * two).astype(jnp.bfloat16)
        mixed[at, 512:768] = (c[3] * one + c[4] * two).astype(jnp.bfloat16)
        mixed[at, 768:1024] = (c[5] * product(k - 2, 3)).astype(jnp.bfloat16)

    copies = []
    blocks = [(k, o) for k in range(SLOTS) for o in range(OPS)]
    mix(*blocks[0], 0)
    for i, (k, o) in enumerate(blocks):
        if i + 1 < len(blocks):
            mix(*blocks[i + 1], (i + 1) % OPS)
        result[o, k] = jnp.dot(tra[k], mixed[i % OPS], preferred_element_type=jnp.float32).astype(jnp.bfloat16)
        copies.append(pltpu.make_async_copy(result.at[o, k], out_ref.at[o, k], sems.at[o, k]))
        copies[-1].start()
    for copy in copies:
        copy.wait()


VMEM, SMEM, ANY, HBM = (pl.BlockSpec(memory_space=m) for m in (pltpu.VMEM, pltpu.SMEM, pl.ANY, pltpu.HBM))


def local(left_env, site_tensor, sec_sizes, coupling_values, coupling_mask):
    buf, halo = pl.pallas_call(
        gather,
        name="gather",
        out_shape=[
            pltpu.VMEM((NX * NZ, SLOTS, 16, 128), jnp.bfloat16),
            pltpu.VMEM((OPS, 2, DIM, DIM), jnp.bfloat16),
        ],
        in_specs=[HBM] * 3,
        out_specs=[VMEM] * 2,
        scratch_shapes=[
            pltpu.VMEM((SLOTS, 16, 128), jnp.bfloat16),
            pltpu.VMEM((SLOTS, 8, DIM), jnp.bfloat16),
            pltpu.SMEM((NB * SLOTS,), jnp.int32),
            pltpu.SemaphoreType.DMA((NX * NZ,)),
            pltpu.SemaphoreType.DMA((NX,)),
            pltpu.SemaphoreType.DMA,
            pltpu.SemaphoreType.DMA((2,)),
            pltpu.SemaphoreType.DMA((2,)),
            pltpu.SemaphoreType.DMA,
            pltpu.SemaphoreType.DMA,
            pltpu.SemaphoreType.DMA((2,)),
        ],
        compiler_params=pltpu.CompilerParams(
            collective_id=0, has_side_effects=True, vmem_limit_bytes=56 * 1024 * 1024
        ),
        cost_estimate=pl.CostEstimate(flops=0, bytes_accessed=6_000_000, transcendentals=0),
    )(left_env, site_tensor, sec_sizes)
    return pl.pallas_call(
        products,
        name="products",
        out_shape=jax.ShapeDtypeStruct(left_env.shape, jnp.bfloat16),
        in_specs=[VMEM, VMEM, VMEM, SMEM, SMEM],
        out_specs=HBM,
        scratch_shapes=[
            pltpu.VMEM((SLOTS, 4, DIM, DIM), jnp.bfloat16),
            pltpu.VMEM((SLOTS, DIM, 4 * DIM), jnp.bfloat16),
            pltpu.VMEM((OPS, 4 * DIM, DIM), jnp.bfloat16),
            pltpu.VMEM((OPS, SLOTS, DIM, DIM), jnp.bfloat16),
            pltpu.SemaphoreType.DMA((OPS, SLOTS)),
        ],
        compiler_params=pltpu.CompilerParams(vmem_limit_bytes=32 * 1024 * 1024),
        cost_estimate=pl.CostEstimate(flops=3_221_225_472, bytes_accessed=3_145_728, transcendentals=0),
    )(left_env, buf, halo, coupling_values, coupling_mask)


def solution(mesh):
    placed = (P("op", "bond", None, None), P("bond", "op", None), P(), P("op", None), P("op", None))
    return jax.shard_map(
        local, mesh=mesh, in_specs=placed, out_specs=P("op", "bond", None, None), check_vma=False
    )
```

```python
import jax
import jax.numpy as jnp
from jax import lax
from jax.experimental import pallas as pl
from jax.experimental.pallas import tpu as pltpu
from jax.sharding import PartitionSpec as P

MESH = pl.DeviceIdType.MESH
NX, NZ, NB = 4, 32, 8
SLOTS, OPS, DIM = 4, 3, 256
ROOT = 15

PLAN = (
    (0, 15, (11, 16, 19, 13, 113, 47, 111, 79)),
    (0, 16, (20, 80, 48, 112)),
    (0, 47, (46, 78)),
    (0, 111, (110,)),
    (0, 13, (12, 77, 45, 109)),
    (0, 79, ()),
    (0, 113, (114, 49, 17, 81)),
    (0, 11, (8, 107, 43)),
    (0, 19, (27, 115, 50, 51)),
    (0, 48, ()),
    (0, 112, ()),
    (0, 46, (14,)),
    (0, 110, ()),
    (0, 80, ()),
    (0, 12, (9, 76, 44, 108)),
    (0, 109, ()),
    (0, 45, ()),
    (0, 78, ()),
    (0, 114, (18, 82)),
    (0, 81, ()),
    (0, 17, ()),
    (0, 20, (21, 84, 52, 116)),
    (0, 77, ()),
    (0, 107, (106,)),
    (0, 43, (75,)),
    (0, 49, ()),
    (0, 115, (83,)),
    (0, 8, (2, 72, 5, 40, 104)),
    (0, 14, ()),
    (0, 51, ()),
    (0, 50, ()),
    (0, 108, ()),
    (0, 44, ()),
    (0, 18, ()),
    (0, 76, ()),
    (0, 82, ()),
    (0, 21, (23, 22, 53, 117)),
    (0, 9, (73, 10, 41, 105)),
    (0, 116, ()),
    (0, 52, ()),
    (0, 106, (42, 74)),
    (0, 83, ()),
    (0, 75, ()),
    (0, 84, (85,)),
    (0, 104, ()),
    (0, 40, ()),
    (0, 72, (71, 7)),
    (0, 27, (29, 58, 123, 26, 28, 59)),
    (0, 53, (54,)),
    (0, 117, ()),
    (0, 5, (69, 4, 6, 37, 101)),
    (0, 22, (118,)),
    (0, 41, ()),
    (0, 105, ()),
    (0, 10, ()),
    (0, 23, (24, 55, 119)),
    (0, 74, ()),
    (0, 73, ()),
    (0, 85, (86,)),
    (0, 42, ()),
    (0, 2, (34, 0, 66, 1, 3, 98)),
    (0, 71, (103,)),
    (0, 123, (91, 122, 124)),
    (0, 28, ()),
    (0, 59, ()),
    (0, 26, (25,)),
    (0, 29, (63, 126, 61, 30, 125)),
    (0, 118, ()),
    (0, 58, (57,)),
    (0, 54, ()),
    (0, 37, ()),
    (0, 4, (36, 100)),
    (0, 101, ()),
    (0, 6, (38,)),
    (0, 55, ()),
    (0, 7, (39,)),
    (0, 119, ()),
    (0, 24, (120, 56)),
    (0, 69, (68, 70)),
    (0, 34, (33,)),
    (0, 86, (87,)),
    (0, 98, ()),
    (0, 1, (97,)),
    (0, 3, (35, 99)),
    (0, 103, (102,)),
    (0, 91, (92,)),
    (0, 122, (90, 121)),
    (0, 124, ()),
    (0, 66, (65, 67)),
    (0, 0, (64, 31, 96)),
    (0, 30, ()),
    (0, 61, (60, 62, 93)),
    (0, 25, ()),
    (0, 125, ()),
    (0, 36, ()),
    (0, 57, (89,)),
    (0, 100, ()),
    (0, 126, (94, 127)),
    (0, 38, ()),
    (0, 68, ()),
    (0, 120, (88,)),
    (0, 63, (95,)),
    (0, 39, ()),
    (0, 33, (32,)),
    (0, 70, ()),
    (0, 97, ()),
    (0, 56, ()),
    (0, 102, ()),
    (0, 87, ()),
    (0, 99, ()),
    (0, 35, ()),
    (0, 121, ()),
    (0, 92, ()),
    (0, 90, ()),
    (0, 31, ()),
    (0, 67, ()),
    (0, 93, ()),
    (0, 96, ()),
    (0, 65, ()),
    (0, 62, ()),
    (0, 89, ()),
    (0, 60, ()),
    (0, 127, ()),
    (0, 64, ()),
    (0, 94, ()),
    (0, 95, ()),
    (0, 32, ()),
    (0, 88, ()),
)


def offset(node):
    return (node // NZ, node % NZ - ROOT)


def gather(
    env_ref, site_in, sizes_in, buf, halo_ref,
    stage, site_ref, sizes_ref,
    recv_sems, leaf_sems, send_sem, own_send, own_recv, halo_send, halo_recv, in_sems,
):
    op, bond = lax.axis_index("op"), lax.axis_index("bond")
    x, z = op // NZ, op % NZ
    shift = (x + 1) // 2
    next_bond = lax.rem(bond + 1, NB)
    last_bond = lax.rem(bond + NB - 1, NB)
    lists = {n: c for _, n, c in PLAN}

    def device(dx, dz, b):
        return (lax.rem(x + dx + 2 * NX, NX) * NZ + lax.rem(z + dz + 2 * NZ, NZ), b)

    first = sorted(lists[ROOT], key=lambda c: -abs(offset(c)[1]))
    barrier = pltpu.get_barrier_semaphore()
    for child in first:
        dx, dz = offset(child)
        for b in (last_bond, bond):
            pl.semaphore_signal(barrier, inc=1, device_id=device(-dx, -dz, b), device_id_type=MESH)
    pl.semaphore_signal(barrier, inc=1, device_id=(op, last_bond), device_id_type=MESH)

    site_copy = pltpu.make_async_copy(site_in, site_ref, in_sems.at[0])
    sizes_copy = pltpu.make_async_copy(sizes_in, sizes_ref, in_sems.at[1])
    for c in (site_copy, sizes_copy):
        c.start()
    site_copy.wait()
    sizes_copy.wait()

    rows = lax.broadcasted_iota(jnp.int32, (8, DIM), 0) + z * 8
    cols = lax.broadcasted_iota(jnp.int32, (8, DIM), 1)
    for k in range(SLOTS):
        at = lax.rem(k - shift + SLOTS, SLOTS)
        left = bond * SLOTS + at
        right = left + shift
        height = sizes_ref[left]
        width = jnp.where(right < NB * SLOTS, sizes_ref[lax.rem(right, NB * SLOTS)], 0)
        block = site_ref[at].astype(jnp.float32)
        block = jnp.where((rows < height) & (cols < width), block, 0.0)
        stage[k] = jnp.concatenate([block[:, :128], block[:, 128:]], axis=0).astype(jnp.bfloat16)

    pl.semaphore_wait(barrier, 2 * len(first) + 1)

    def arrival(child):
        return recv_sems.at[child] if lists[child] else leaf_sems.at[child // NZ]

    for moved in range(3):
        @pl.when(shift == moved)
        def _():
            for child in lists[ROOT]:
                dx, dz = offset(child)
                for lo, hi, to in ((0, moved, next_bond), (moved, SLOTS, bond)):
                    if lo < hi:
                        pltpu.make_async_remote_copy(
                            src_ref=stage.at[pl.ds(lo, hi - lo)],
                            dst_ref=buf.at[child, pl.ds(lo, hi - lo)],
                            send_sem=send_sem, recv_sem=arrival(child),
                            device_id=device(dx, dz, to), device_id_type=MESH,
                        ).start()

    def own_copy(k):
        return pltpu.make_async_remote_copy(
            src_ref=stage.at[k], dst_ref=buf.at[ROOT, k],
            send_sem=own_send.at[k], recv_sem=own_recv.at[k],
            device_id=(op, next_bond), device_id_type=MESH,
        )

    halo = pltpu.make_async_remote_copy(
        src_ref=env_ref.at[:, 2:4], dst_ref=halo_ref,
        send_sem=halo_send, recv_sem=halo_recv,
        device_id=(op, next_bond), device_id_type=MESH,
    )
    for k in range(SLOTS):
        if k < 2:
            @pl.when(k < shift)
            def _():
                own_copy(k).start()

            @pl.when(k >= shift)
            def _():
                buf[ROOT, k] = stage[k]
        else:
            buf[ROOT, k] = stage[k]
    halo.start()

    def copy(node, child):
        (ax, az), (bx, bz) = offset(node), offset(child)
        return pltpu.make_async_remote_copy(
            src_ref=buf.at[node], dst_ref=buf.at[child],
            send_sem=send_sem, recv_sem=arrival(child),
            device_id=device(bx - ax, bz - az, bond), device_id_type=MESH,
        )

    for _, node, children in PLAN:
        if node != ROOT and children:
            copy(node, node).wait_recv()
            for child in children:
                copy(node, child).start()

    for k in range(2):
        @pl.when(k < shift)
        def _():
            own_copy(k).wait_recv()

    for ox in range(NX):
        leaves = sum(1 for n, c in lists.items() if n // NZ == ox and not c)
        if leaves:
            some = buf.at[pl.ds(0, leaves)]
            pltpu.make_async_remote_copy(
                src_ref=some, dst_ref=some, send_sem=send_sem, recv_sem=leaf_sems.at[ox],
                device_id=(op, next_bond), device_id_type=MESH,
            ).wait_recv()
    halo.wait_recv()
    for k in range(2):
        @pl.when(k < shift)
        def _():
            own_copy(k).wait_send()
    halo.wait_send()
    everything = buf.at[pl.ds(0, NX * NZ - 1)]
    pltpu.make_async_remote_copy(
        src_ref=everything, dst_ref=everything, send_sem=send_sem, recv_sem=halo_recv,
        device_id=(op, next_bond), device_id_type=MESH,
    ).wait_send()


def products(own, buf, halo, values_ref, mask_ref, out_ref, nat, tra, mixed, result, sems):
    op = lax.axis_index("op")
    x, z = op // NZ, op % NZ
    tile = [lax.rem(z + ROOT - m + NZ, NZ) for m in range(NZ)]
    plane = [lax.rem(x - s + NX, NX) * NZ for s in range(4)]
    for k in range(SLOTS):
        for s in range(4):
            tiles = [buf[plane[s] + j, k].astype(jnp.float32) for j in tile]
            left = jnp.concatenate([t[:8] for t in tiles], axis=0)
            right = jnp.concatenate([t[8:] for t in tiles], axis=0)
            block = jnp.concatenate([left, right], axis=1).astype(jnp.bfloat16)
            nat[k, s] = block
            tra[k, :, s * DIM:(s + 1) * DIM] = block.T

    def env(o, e):
        return own[o, e] if e >= 0 else halo[o, e + 2]

    def mix(k, o, at):
        c = [values_ref[o, q] * mask_ref[o, q].astype(jnp.float32) for q in range(6)]

        def product(e, s):
            return jnp.dot(env(o, e), nat[k, s], preferred_element_type=jnp.float32)

        mixed[at, 0:256] = (c[0] * product(k, 0)).astype(jnp.bfloat16)
        one, two = product(k - 1, 1), product(k - 1, 2)
        mixed[at, 256:512] = (c[1] * one + c[2] * two).astype(jnp.bfloat16)
        mixed[at, 512:768] = (c[3] * one + c[4] * two).astype(jnp.bfloat16)
        mixed[at, 768:1024] = (c[5] * product(k - 2, 3)).astype(jnp.bfloat16)

    copies = []
    blocks = [(k, o) for k in range(SLOTS) for o in range(OPS)]
    mix(*blocks[0], 0)
    for i, (k, o) in enumerate(blocks):
        if i + 1 < len(blocks):
            mix(*blocks[i + 1], (i + 1) % OPS)
        result[o, k] = jnp.dot(tra[k], mixed[i % OPS], preferred_element_type=jnp.float32).astype(jnp.bfloat16)
        copies.append(pltpu.make_async_copy(result.at[o, k], out_ref.at[o, k], sems.at[o, k]))
        copies[-1].start()
    for copy in copies:
        copy.wait()


VMEM, SMEM, ANY, HBM = (pl.BlockSpec(memory_space=m) for m in (pltpu.VMEM, pltpu.SMEM, pl.ANY, pltpu.HBM))


def local(left_env, site_tensor, sec_sizes, coupling_values, coupling_mask):
    buf, halo = pl.pallas_call(
        gather,
        name="gather",
        out_shape=[
            pltpu.VMEM((NX * NZ, SLOTS, 16, 128), jnp.bfloat16),
            pltpu.VMEM((OPS, 2, DIM, DIM), jnp.bfloat16),
        ],
        in_specs=[HBM] * 3,
        out_specs=[VMEM] * 2,
        scratch_shapes=[
            pltpu.VMEM((SLOTS, 16, 128), jnp.bfloat16),
            pltpu.VMEM((SLOTS, 8, DIM), jnp.bfloat16),
            pltpu.SMEM((NB * SLOTS,), jnp.int32),
            pltpu.SemaphoreType.DMA((NX * NZ,)),
            pltpu.SemaphoreType.DMA((NX,)),
            pltpu.SemaphoreType.DMA,
            pltpu.SemaphoreType.DMA((2,)),
            pltpu.SemaphoreType.DMA((2,)),
            pltpu.SemaphoreType.DMA,
            pltpu.SemaphoreType.DMA,
            pltpu.SemaphoreType.DMA((2,)),
        ],
        compiler_params=pltpu.CompilerParams(
            collective_id=0, has_side_effects=True, vmem_limit_bytes=56 * 1024 * 1024
        ),
        cost_estimate=pl.CostEstimate(flops=0, bytes_accessed=6_000_000, transcendentals=0),
    )(left_env, site_tensor, sec_sizes)
    return pl.pallas_call(
        products,
        name="products",
        out_shape=jax.ShapeDtypeStruct(left_env.shape, jnp.bfloat16),
        in_specs=[VMEM, VMEM, VMEM, SMEM, SMEM],
        out_specs=HBM,
        scratch_shapes=[
            pltpu.VMEM((SLOTS, 4, DIM, DIM), jnp.bfloat16),
            pltpu.VMEM((SLOTS, DIM, 4 * DIM), jnp.bfloat16),
            pltpu.VMEM((OPS, 4 * DIM, DIM), jnp.bfloat16),
            pltpu.VMEM((OPS, SLOTS, DIM, DIM), jnp.bfloat16),
            pltpu.SemaphoreType.DMA((OPS, SLOTS)),
        ],
        compiler_params=pltpu.CompilerParams(vmem_limit_bytes=32 * 1024 * 1024),
        cost_estimate=pl.CostEstimate(flops=3_221_225_472, bytes_accessed=3_145_728, transcendentals=0),
    )(left_env, buf, halo, coupling_values, coupling_mask)


def solution(mesh):
    placed = (P("op", "bond", None, None), P("bond", "op", None), P(), P("op", None), P("op", None))
    return jax.shard_map(
        local, mesh=mesh, in_specs=placed, out_specs=P("op", "bond", None, None), check_vma=False
    )
```

```python
import jax
import jax.numpy as jnp
from jax import lax
from jax.experimental import pallas as pl
from jax.experimental.pallas import tpu as pltpu
from jax.sharding import PartitionSpec as P

MESH = pl.DeviceIdType.MESH
NX, NZ, NB = 4, 32, 8
SLOTS, OPS, DIM = 4, 3, 256
ROOT = 15

PLAN = (
    (0, 15, (11, 16, 19, 13, 113, 47, 111, 79)),
    (0, 16, (20, 80, 48, 112)),
    (0, 47, (46,)),
    (0, 111, (78, 110)),
    (0, 13, (12, 45, 109)),
    (0, 79, ()),
    (0, 113, (114, 49, 17, 81)),
    (0, 11, (8, 107, 43)),
    (0, 48, ()),
    (0, 112, ()),
    (0, 46, (14,)),
    (0, 19, (27, 115, 50, 51)),
    (0, 110, ()),
    (0, 80, ()),
    (0, 12, (9, 108, 44)),
    (0, 45, (77,)),
    (0, 109, ()),
    (0, 78, ()),
    (0, 114, (18, 82)),
    (0, 17, ()),
    (0, 81, ()),
    (0, 20, (21, 84, 52, 116)),
    (0, 43, (75,)),
    (0, 107, (106,)),
    (0, 49, ()),
    (0, 115, (83,)),
    (0, 8, (2, 72, 5, 40, 104)),
    (0, 14, ()),
    (0, 51, ()),
    (0, 50, ()),
    (0, 108, (76,)),
    (0, 44, ()),
    (0, 77, ()),
    (0, 82, ()),
    (0, 18, ()),
    (0, 116, ()),
    (0, 21, (23, 22, 53, 117)),
    (0, 106, (42, 74)),
    (0, 52, ()),
    (0, 9, (73, 10, 41, 105)),
    (0, 75, ()),
    (0, 83, ()),
    (0, 84, (85,)),
    (0, 104, ()),
    (0, 40, ()),
    (0, 76, ()),
    (0, 72, (71, 7)),
    (0, 27, (29, 58, 123, 26, 28, 59)),
    (0, 53, (54,)),
    (0, 117, ()),
    (0, 5, (69, 4, 6, 37, 101)),
    (0, 22, (118,)),
    (0, 74, ()),
    (0, 10, ()),
    (0, 41, ()),
    (0, 23, (24, 55, 119)),
    (0, 105, ()),
    (0, 42, ()),
    (0, 85, (86,)),
    (0, 73, ()),
    (0, 2, (34, 0, 66, 1, 3, 98)),
    (0, 71, (103,)),
    (0, 123, (91, 122, 124)),
    (0, 28, ()),
    (0, 59, ()),
    (0, 26, (25,)),
    (0, 29, (63, 126, 61, 30, 125)),
    (0, 118, ()),
    (0, 58, (57,)),
    (0, 6, (38,)),
    (0, 37, ()),
    (0, 4, (36, 100)),
    (0, 101, ()),
    (0, 54, ()),
    (0, 55, ()),
    (0, 7, (39,)),
    (0, 119, ()),
    (0, 24, (120, 56)),
    (0, 69, (68, 70)),
    (0, 34, (33,)),
    (0, 86, (87,)),
    (0, 98, ()),
    (0, 1, (97,)),
    (0, 3, (35, 99)),
    (0, 103, (102,)),
    (0, 91, (92,)),
    (0, 122, (90, 121)),
    (0, 124, ()),
    (0, 66, (65, 67)),
    (0, 0, (64, 31, 96)),
    (0, 30, ()),
    (0, 61, (60, 62, 93)),
    (0, 25, ()),
    (0, 125, ()),
    (0, 36, ()),
    (0, 57, (89,)),
    (0, 126, (94, 127)),
    (0, 100, ()),
    (0, 38, ()),
    (0, 68, ()),
    (0, 63, (95,)),
    (0, 120, (88,)),
    (0, 39, ()),
    (0, 33, (32,)),
    (0, 70, ()),
    (0, 97, ()),
    (0, 56, ()),
    (0, 102, ()),
    (0, 87, ()),
    (0, 99, ()),
    (0, 35, ()),
    (0, 121, ()),
    (0, 92, ()),
    (0, 90, ()),
    (0, 31, ()),
    (0, 67, ()),
    (0, 93, ()),
    (0, 96, ()),
    (0, 65, ()),
    (0, 62, ()),
    (0, 89, ()),
    (0, 60, ()),
    (0, 64, ()),
    (0, 127, ()),
    (0, 94, ()),
    (0, 95, ()),
    (0, 32, ()),
    (0, 88, ()),
)


def offset(node):
    return (node // NZ, node % NZ - ROOT)


def gather(
    env_ref, site_in, sizes_in, buf, halo_ref,
    stage, site_ref, sizes_ref,
    recv_sems, leaf_sems, send_sem, own_send, own_recv, halo_send, halo_recv, in_sems,
):
    op, bond = lax.axis_index("op"), lax.axis_index("bond")
    x, z = op // NZ, op % NZ
    shift = (x + 1) // 2
    next_bond = lax.rem(bond + 1, NB)
    last_bond = lax.rem(bond + NB - 1, NB)
    lists = {n: c for _, n, c in PLAN}

    def device(dx, dz, b):
        return (lax.rem(x + dx + 2 * NX, NX) * NZ + lax.rem(z + dz + 2 * NZ, NZ), b)

    first = sorted(lists[ROOT], key=lambda c: -abs(offset(c)[1]))
    barrier = pltpu.get_barrier_semaphore()
    for child in first:
        dx, dz = offset(child)
        for b in (last_bond, bond):
            pl.semaphore_signal(barrier, inc=1, device_id=device(-dx, -dz, b), device_id_type=MESH)
    pl.semaphore_signal(barrier, inc=1, device_id=(op, last_bond), device_id_type=MESH)

    site_copy = pltpu.make_async_copy(site_in, site_ref, in_sems.at[0])
    sizes_copy = pltpu.make_async_copy(sizes_in, sizes_ref, in_sems.at[1])
    for c in (site_copy, sizes_copy):
        c.start()
    site_copy.wait()
    sizes_copy.wait()

    rows = lax.broadcasted_iota(jnp.int32, (8, DIM), 0) + z * 8
    cols = lax.broadcasted_iota(jnp.int32, (8, DIM), 1)
    for k in range(SLOTS):
        at = lax.rem(k - shift + SLOTS, SLOTS)
        left = bond * SLOTS + at
        right = left + shift
        height = sizes_ref[left]
        width = jnp.where(right < NB * SLOTS, sizes_ref[lax.rem(right, NB * SLOTS)], 0)
        block = site_ref[at].astype(jnp.float32)
        block = jnp.where((rows < height) & (cols < width), block, 0.0)
        stage[k] = jnp.concatenate([block[:, :128], block[:, 128:]], axis=0).astype(jnp.bfloat16)

    pl.semaphore_wait(barrier, 2 * len(first) + 1)

    def arrival(child):
        return recv_sems.at[child] if lists[child] else leaf_sems.at[child // NZ]

    for moved in range(3):
        @pl.when(shift == moved)
        def _():
            for child in lists[ROOT]:
                dx, dz = offset(child)
                for lo, hi, to in ((0, moved, next_bond), (moved, SLOTS, bond)):
                    if lo < hi:
                        pltpu.make_async_remote_copy(
                            src_ref=stage.at[pl.ds(lo, hi - lo)],
                            dst_ref=buf.at[child, pl.ds(lo, hi - lo)],
                            send_sem=send_sem, recv_sem=arrival(child),
                            device_id=device(dx, dz, to), device_id_type=MESH,
                        ).start()

    def own_copy(k):
        return pltpu.make_async_remote_copy(
            src_ref=stage.at[k], dst_ref=buf.at[ROOT, k],
            send_sem=own_send.at[k], recv_sem=own_recv.at[k],
            device_id=(op, next_bond), device_id_type=MESH,
        )

    halo = pltpu.make_async_remote_copy(
        src_ref=env_ref.at[:, 2:4], dst_ref=halo_ref,
        send_sem=halo_send, recv_sem=halo_recv,
        device_id=(op, next_bond), device_id_type=MESH,
    )
    for k in range(SLOTS):
        if k < 2:
            @pl.when(k < shift)
            def _():
                own_copy(k).start()

            @pl.when(k >= shift)
            def _():
                buf[ROOT, k] = stage[k]
        else:
            buf[ROOT, k] = stage[k]
    halo.start()

    def copy(node, child):
        (ax, az), (bx, bz) = offset(node), offset(child)
        return pltpu.make_async_remote_copy(
            src_ref=buf.at[node], dst_ref=buf.at[child],
            send_sem=send_sem, recv_sem=arrival(child),
            device_id=device(bx - ax, bz - az, bond), device_id_type=MESH,
        )

    for _, node, children in PLAN:
        if node != ROOT and children:
            copy(node, node).wait_recv()
            for child in children:
                copy(node, child).start()

    for k in range(2):
        @pl.when(k < shift)
        def _():
            own_copy(k).wait_recv()

    for ox in range(NX):
        leaves = sum(1 for n, c in lists.items() if n // NZ == ox and not c)
        if leaves:
            some = buf.at[pl.ds(0, leaves)]
            pltpu.make_async_remote_copy(
                src_ref=some, dst_ref=some, send_sem=send_sem, recv_sem=leaf_sems.at[ox],
                device_id=(op, next_bond), device_id_type=MESH,
            ).wait_recv()
    halo.wait_recv()
    for k in range(2):
        @pl.when(k < shift)
        def _():
            own_copy(k).wait_send()
    halo.wait_send()
    everything = buf.at[pl.ds(0, NX * NZ - 1)]
    pltpu.make_async_remote_copy(
        src_ref=everything, dst_ref=everything, send_sem=send_sem, recv_sem=halo_recv,
        device_id=(op, next_bond), device_id_type=MESH,
    ).wait_send()


def products(own, buf, halo, values_ref, mask_ref, out_ref, nat, tra, mixed, result, sems):
    op = lax.axis_index("op")
    x, z = op // NZ, op % NZ
    tile = [lax.rem(z + ROOT - m + NZ, NZ) for m in range(NZ)]
    plane = [lax.rem(x - s + NX, NX) * NZ for s in range(4)]
    for k in range(SLOTS):
        for s in range(4):
            tiles = [buf[plane[s] + j, k].astype(jnp.float32) for j in tile]
            left = jnp.concatenate([t[:8] for t in tiles], axis=0)
            right = jnp.concatenate([t[8:] for t in tiles], axis=0)
            block = jnp.concatenate([left, right], axis=1).astype(jnp.bfloat16)
            nat[k, s] = block
            tra[k, :, s * DIM:(s + 1) * DIM] = block.T

    def env(o, e):
        return own[o, e] if e >= 0 else halo[o, e + 2]

    def mix(k, o, at):
        c = [values_ref[o, q] * mask_ref[o, q].astype(jnp.float32) for q in range(6)]

        def product(e, s):
            return jnp.dot(env(o, e), nat[k, s], preferred_element_type=jnp.float32)

        mixed[at, 0:256] = (c[0] * product(k, 0)).astype(jnp.bfloat16)
        one, two = product(k - 1, 1), product(k - 1, 2)
        mixed[at, 256:512] = (c[1] * one + c[2] * two).astype(jnp.bfloat16)
        mixed[at, 512:768] = (c[3] * one + c[4] * two).astype(jnp.bfloat16)
        mixed[at, 768:1024] = (c[5] * product(k - 2, 3)).astype(jnp.bfloat16)

    copies = []
    blocks = [(k, o) for k in range(SLOTS) for o in range(OPS)]
    mix(*blocks[0], 0)
    for i, (k, o) in enumerate(blocks):
        if i + 1 < len(blocks):
            mix(*blocks[i + 1], (i + 1) % OPS)
        result[o, k] = jnp.dot(tra[k], mixed[i % OPS], preferred_element_type=jnp.float32).astype(jnp.bfloat16)
        copies.append(pltpu.make_async_copy(result.at[o, k], out_ref.at[o, k], sems.at[o, k]))
        copies[-1].start()
    for copy in copies:
        copy.wait()


VMEM, SMEM, ANY, HBM = (pl.BlockSpec(memory_space=m) for m in (pltpu.VMEM, pltpu.SMEM, pl.ANY, pltpu.HBM))


def local(left_env, site_tensor, sec_sizes, coupling_values, coupling_mask):
    buf, halo = pl.pallas_call(
        gather,
        name="gather",
        out_shape=[
            pltpu.VMEM((NX * NZ, SLOTS, 16, 128), jnp.bfloat16),
            pltpu.VMEM((OPS, 2, DIM, DIM), jnp.bfloat16),
        ],
        in_specs=[HBM] * 3,
        out_specs=[VMEM] * 2,
        scratch_shapes=[
            pltpu.VMEM((SLOTS, 16, 128), jnp.bfloat16),
            pltpu.VMEM((SLOTS, 8, DIM), jnp.bfloat16),
            pltpu.SMEM((NB * SLOTS,), jnp.int32),
            pltpu.SemaphoreType.DMA((NX * NZ,)),
            pltpu.SemaphoreType.DMA((NX,)),
            pltpu.SemaphoreType.DMA,
            pltpu.SemaphoreType.DMA((2,)),
            pltpu.SemaphoreType.DMA((2,)),
            pltpu.SemaphoreType.DMA,
            pltpu.SemaphoreType.DMA,
            pltpu.SemaphoreType.DMA((2,)),
        ],
        compiler_params=pltpu.CompilerParams(
            collective_id=0, has_side_effects=True, vmem_limit_bytes=56 * 1024 * 1024
        ),
        cost_estimate=pl.CostEstimate(flops=0, bytes_accessed=6_000_000, transcendentals=0),
    )(left_env, site_tensor, sec_sizes)
    return pl.pallas_call(
        products,
        name="products",
        out_shape=jax.ShapeDtypeStruct(left_env.shape, jnp.bfloat16),
        in_specs=[VMEM, VMEM, VMEM, SMEM, SMEM],
        out_specs=HBM,
        scratch_shapes=[
            pltpu.VMEM((SLOTS, 4, DIM, DIM), jnp.bfloat16),
            pltpu.VMEM((SLOTS, DIM, 4 * DIM), jnp.bfloat16),
            pltpu.VMEM((OPS, 4 * DIM, DIM), jnp.bfloat16),
            pltpu.VMEM((OPS, SLOTS, DIM, DIM), jnp.bfloat16),
            pltpu.SemaphoreType.DMA((OPS, SLOTS)),
        ],
        compiler_params=pltpu.CompilerParams(vmem_limit_bytes=32 * 1024 * 1024),
        cost_estimate=pl.CostEstimate(flops=3_221_225_472, bytes_accessed=3_145_728, transcendentals=0),
    )(left_env, buf, halo, coupling_values, coupling_mask)


def solution(mesh):
    placed = (P("op", "bond", None, None), P("bond", "op", None), P(), P("op", None), P("op", None))
    return jax.shard_map(
        local, mesh=mesh, in_specs=placed, out_specs=P("op", "bond", None, None), check_vma=False
    )
```
